32 devices in a mesh: row: 4 (over y, core), col: 8 (over z, x).
Axes of the slice: x: 2, y: 2, z: 4, core: 2. Of those that a mesh axis runs over, the one named last changes fastest.
Arguments:
- hidden_states: bfloat16 [512, 2048], P('col', 'row'), may hold values from -20 to 20
- input_gain: float32 [2, 2048], P(None, 'row'), may hold values from 0.25 to 1.75
- inner_weight: bfloat16 [2, 2048, 2, 4096], P(None, 'row', None, 'col'), may hold values from -0.125 to 0.125
- proj_weight: bfloat16 [2, 2048, 256], P(None, 'row'), may hold values from -0.125 to 0.125
- step_weight: bfloat16 [2, 2048, 64], P(None, 'row', 'col'), may hold values from -0.125 to 0.125
- inner_kernel: float32 [2, 4, 4096], P(None, None, 'col'), may hold values from -3 to 3
- proj_kernel: float32 [2, 4, 256], replicated, may hold values from -3 to 3
- step_bias: float32 [2, 64], P(None, 'col'), may hold values from -5 to -1
- decay_log: float32 [2, 64], P(None, 'col'), may hold values from -2 to 1
- skip_gain: float32 [2, 64], P(None, 'col'), may hold values from 0.5 to 1.5
- norm_gain: float32 [2, 4096], P(None, 'col'), may hold values from 0.25 to 1.75
- out_weight: bfloat16 [2, 4096, 2048], P(None, 'col', 'row'), may hold values from -0.09375 to 0.09375
- inner_cache: bfloat16 [2, 32, 3, 4096], P(None, 'row', None, 'col'), may hold values from -6 to 6
- proj_cache: bfloat16 [2, 32, 3, 256], P(None, 'row'), may hold values from -6 to 6
- state_cache: float32 [2, 32, 64, 64, 128], P(None, 'row', 'col'), may hold values from -1.2 to 1.2
- accepted: int32 [32], P('row'), may hold values from 1 to 16
- owners: int32 [32], P('row'), may hold values from 0 to 7, as said below
- tenant_ranges: int32 [4, 2], replicated, may hold values from 0 to 32, as said below
Outputs:
- hidden_output: bfloat16 [512, 2048], P('col', 'row')
- step_states: bfloat16 [2, 32, 16, 64, 64, 128], P(None, 'row', None, 'col')
- owned_states: bfloat16 [4, 8, 2, 2, 64, 64, 128], P('row', 'col')
The draws below stay inside these ranges and needn't reach their ends.
Inputs may be any that keep to these rules, and one draw needn't show every extreme that they name: `owners`: within the requests of one index of row (aligned blocks of 8) no owner appears more than 2 times, and in every block some owner appears exactly 2 times. `tenant_ranges`: the ranges are in order, disjoint and not empty; exactly 4 requests lie in no range.
All inputs are finite; a program needn't handle non-finite values.
Results may differ from the reference program's by a relative error of at most 0.024.
Values may be sent and summed in bfloat16 or wider, within the bound.
A program may use at most 192 MiB of HBM per device.

```python
import jax
import jax.numpy as jnp
from jax import lax

D = 2048
H = 64
P_SIZE = 64
N = 128
K = 4
L = 2
S = 16
TENANTS = 4
SEND_CAP = 2
REQ_ROW = 8
DI = 4096
REQ = 32
TOK = 512
GROUPS = 4
OWNERS = 8


def draw_hidden_states(key, part):
    first_key = jax.random.fold_in(key, 0)
    column_scale = 0.5 + jnp.arange(D, dtype=jnp.float32) / D
    drawn = jax.random.truncated_normal(first_key, -4.0, 4.0, (TOK, D), jnp.float32) * column_scale
    return drawn.astype(jnp.bfloat16)


def draw_owners(key, part):

    def one_block(block_key):
        sub_keys = jax.random.split(block_key, 3)
        shuffled = jax.random.permutation(sub_keys[0], OWNERS).astype(jnp.int32)
        others = jnp.repeat(shuffled[1:], SEND_CAP, total_repeat_length=(OWNERS - 1) * SEND_CAP)
        others = jax.random.permutation(sub_keys[1], others)
        listing = jnp.concatenate([jnp.full((SEND_CAP,), shuffled[0], dtype=jnp.int32), others.astype(jnp.int32)])[:REQ_ROW]
        return jax.random.permutation(sub_keys[2], listing)
    block_keys = jax.random.split(key, GROUPS)
    return jax.vmap(one_block)(block_keys).reshape(REQ).astype(jnp.int32)


def composition(key, amount, pieces):
    cut_points = jnp.sort(jax.random.randint(key, (pieces - 1,), 0, amount + 1))
    edge_points = jnp.concatenate([jnp.zeros((1,), jnp.int32), cut_points.astype(jnp.int32), jnp.full((1,), amount, jnp.int32)])
    return edge_points[1:] - edge_points[:-1]


def draw_tenant_ranges(key, part):
    dead_count = REQ // 8
    live_count = REQ - dead_count
    first_key, second_key = jax.random.split(key)
    lengths = composition(first_key, live_count - TENANTS, TENANTS) + 1
    gap_sizes = composition(second_key, dead_count, TENANTS + 1)
    starts = jnp.cumsum(gap_sizes[:TENANTS]) + jnp.concatenate([jnp.zeros((1,), jnp.int32), jnp.cumsum(lengths)[:-1].astype(jnp.int32)])
    end_points = starts + lengths
    return jnp.stack([starts, end_points], axis=1).astype(jnp.int32)


def plant(array, key, least, high):
    dims = array.shape
    place = [jax.random.randint(jax.random.fold_in(key, axis), (), 0, dims[axis]) for axis in range(len(dims))]
    array = array.at[tuple(place)].set(least)
    longest = dims.index(max(dims))
    place[longest] = (place[longest] + 1) % dims[longest]
    return array.at[tuple(place)].set(high)


def steps_of(key, extent, shards, smallest, largest):
    def one(axis_at, shards_of):
        steps = jax.random.uniform(jax.random.fold_in(jax.random.fold_in(key, 6), axis_at), (shards_of,), jnp.float32, smallest / len(shards), largest / len(shards))
        return jnp.repeat(jnp.exp(steps), extent[axis_at] // shards_of).reshape((-1,) + (1,) * (len(extent) - axis_at - 1))

    factor_of = one(*shards[0])
    for cut in shards[1:]:
        factor_of = factor_of * one(*cut)
    return factor_of


def scatter_about(own_key, extent, scale, most, cuts=(), kind=jnp.bfloat16):
    array = scale * jax.random.normal(own_key, extent, jnp.float32)
    if cuts:
        array = array * steps_of(own_key, extent, cuts, -0.22, 0.18)
    return jnp.clip(array, -most, most).astype(kind)


def setup_inputs(seed: int = 0) -> dict:
    keys = jax.random.split(jax.random.key(seed), 19)
    return {
        "hidden_states": draw_hidden_states(jax.random.fold_in(keys[18], 71), 0),
        "input_gain": jnp.clip(1.0 + 0.15 * jax.random.normal(keys[1], (L, D), jnp.float32), 0.25, 1.75),
        "inner_weight": scatter_about(keys[2], (L, D, 2, DI), D ** -0.5, 0.125, ((1, 4), (3, 8))),
        "proj_weight": scatter_about(keys[3], (L, D, 2 * N), D ** -0.5, 0.125, ((1, 4),)),
        "step_weight": scatter_about(keys[4], (L, D, H), D ** -0.5, 0.125, ((1, 4), (2, 8))),
        "inner_kernel": scatter_about(keys[5], (L, K, DI), K ** -0.5, 3.0, ((2, 8),), jnp.float32),
        "proj_kernel": scatter_about(keys[6], (L, K, 2 * N), K ** -0.5, 3.0, (), jnp.float32),
        "step_bias": jnp.clip(-5.0 + 4.0 * jax.random.uniform(keys[7], (L, H), jnp.float32) ** steps_of(keys[7], (L, H), ((1, 8),), -0.2, 0.2), -5.0, -1.0),
        "decay_log": jnp.clip(-2.0 + 3.0 * jax.random.uniform(keys[8], (L, H), jnp.float32) ** steps_of(keys[8], (L, H), ((1, 8),), -0.2, 0.2), -2.0, 1.0),
        "skip_gain": jnp.clip(0.5 + 1.0 * jax.random.uniform(keys[9], (L, H), jnp.float32) ** steps_of(keys[9], (L, H), ((1, 8),), -0.2, 0.2), 0.5, 1.5),
        "norm_gain": jnp.clip(1.0 + 0.15 * jax.random.normal(keys[10], (L, DI), jnp.float32), 0.25, 1.75),
        "out_weight": scatter_about(keys[11], (L, DI, D), DI ** -0.5, 0.09375, ((1, 8), (2, 4))),
        "inner_cache": scatter_about(keys[12], (L, REQ, K - 1, DI), 1.0, 6.0, ((1, 4), (3, 8))),
        "proj_cache": scatter_about(keys[13], (L, REQ, K - 1, 2 * N), 1.0, 6.0, ((1, 4),)),
        "state_cache": scatter_about(keys[14], (L, REQ, H, P_SIZE, N), 0.2, 1.2, ((1, 4), (2, 8)), jnp.float32),
        "accepted": plant(jax.random.randint(keys[15], (REQ,), 1, S + 1), jax.random.fold_in(keys[15], 1), 1, S).astype(jnp.int32),
        "owners": draw_owners(jax.random.fold_in(keys[18], 71), 0),
        "tenant_ranges": draw_tenant_ranges(jax.random.fold_in(keys[18], 71), 0),
    }


EPSILON = 1e-05

def conv_silu(prefix, incoming, kernel):
    joined = jnp.concatenate([prefix, incoming], axis=1)
    length = incoming.shape[1]
    summed = joined[:, 0:length, :] * kernel[0]
    for offset in range(1, kernel.shape[0]):
        summed = summed + joined[:, offset:offset + length, :] * kernel[offset]
    return jax.nn.silu(summed)

def ssm_scan(decays, deltas, inner_values, b_values, c_values, skip_values, start_state):

    def advance(carried, packed):
        decay_now, delta_now, value_now, b_now, c_now = packed
        updated = decay_now[:, :, None, None] * carried + (delta_now[:, :, None] * value_now)[:, :, :, None] * b_now[:, None, None, :]
        output = jnp.einsum('rhpn,rn->rhp', updated, c_now, precision=lax.Precision.HIGHEST) + skip_values[None, :, None] * value_now
        return (updated, (output, updated.astype(jnp.bfloat16)))
    time_major = tuple((jnp.moveaxis(member, 1, 0) for member in (decays, deltas, inner_values, b_values, c_values)))
    last_state, (outputs, states) = lax.scan(advance, start_state, time_major)
    return (jnp.moveaxis(outputs, 0, 1), jnp.moveaxis(states, 0, 1))

def mamba_layer(hidden, input_gain, inner_weight, proj_weight, step_weight, inner_kernel, proj_kernel, step_bias, decay_log, skip_gain, norm_gain, out_weight, inner_cache, proj_cache, state_cache):
    requests = state_cache.shape[0]
    tokens_f = hidden.astype(jnp.float32)
    inverse_rms = lax.rsqrt(lax.optimization_barrier(jnp.sum(tokens_f * tokens_f, axis=1)) / D + EPSILON)
    scaled = (tokens_f * input_gain).astype(jnp.bfloat16)
    inner_vals = jnp.dot(scaled, inner_weight.reshape(D, 2 * DI), preferred_element_type=jnp.float32) * inverse_rms[:, None]
    proj_vals = jnp.dot(scaled, proj_weight, preferred_element_type=jnp.float32) * inverse_rms[:, None]
    step_vals = jnp.dot(scaled, step_weight, preferred_element_type=jnp.float32) * inverse_rms[:, None]
    gate_vals = inner_vals[:, :DI]
    raw_inner = inner_vals[:, DI:].reshape(requests, S, DI)
    raw_proj = proj_vals.reshape(requests, S, 2 * N)
    conv_inner = conv_silu(inner_cache.astype(jnp.float32), raw_inner, inner_kernel)
    conv_proj = conv_silu(proj_cache.astype(jnp.float32), raw_proj, proj_kernel)
    deltas = jax.nn.softplus(step_vals.reshape(requests, S, H) + step_bias)
    decays = jnp.exp(-deltas * jnp.exp(decay_log))
    outputs, states = ssm_scan(decays, deltas, conv_inner.reshape(requests, S, H, P_SIZE), conv_proj[..., :N], conv_proj[..., N:], skip_gain, state_cache)
    gated_raw = outputs.reshape(requests * S, DI) * jax.nn.silu(gate_vals)
    gate_square = lax.optimization_barrier(jnp.sum(gated_raw * gated_raw, axis=1))
    gated = (gated_raw * norm_gain * lax.rsqrt(gate_square / DI + EPSILON)[:, None]).astype(jnp.bfloat16)
    result = (tokens_f + jnp.dot(gated, out_weight, preferred_element_type=jnp.float32)).astype(jnp.bfloat16)
    return (result, states)

def reference(hidden_states, input_gain, inner_weight, proj_weight, step_weight, inner_kernel, proj_kernel, step_bias, decay_log, skip_gain, norm_gain, out_weight, inner_cache, proj_cache, state_cache, accepted, owners, tenant_ranges):
    hidden = hidden_states
    request_ids = jnp.arange(REQ, dtype=jnp.int32)
    step_list = []
    chosen_list = []
    for layer_index in range(L):
        hidden, states = mamba_layer(hidden, input_gain[layer_index], inner_weight[layer_index], proj_weight[layer_index], step_weight[layer_index], inner_kernel[layer_index], proj_kernel[layer_index], step_bias[layer_index], decay_log[layer_index], skip_gain[layer_index], norm_gain[layer_index], out_weight[layer_index], inner_cache[layer_index], proj_cache[layer_index], state_cache[layer_index])
        step_list.append(states)
        chosen_list.append(states[request_ids, (accepted - 1).astype(jnp.int32)])
    live_mask = jnp.any((request_ids[:, None] >= tenant_ranges[None, :, 0]) & (request_ids[:, None] < tenant_ranges[None, :, 1]), axis=1)
    block_ids = (request_ids // REQ_ROW).astype(jnp.int32)
    earlier = (owners[:, None] == owners[None, :]) & (block_ids[:, None] == block_ids[None, :]) & (request_ids[None, :] < request_ids[:, None])
    slot_ranks = lax.optimization_barrier(jnp.sum(earlier.astype(jnp.int32), axis=1)).astype(jnp.int32)
    chosen_all = jnp.stack(chosen_list, axis=1)
    chosen_all = jnp.where(live_mask[:, None, None, None, None], chosen_all, jnp.zeros_like(chosen_all))
    owned_states = jnp.zeros((GROUPS, OWNERS, SEND_CAP, L, H, P_SIZE, N), jnp.bfloat16).at[block_ids, owners, slot_ranks].set(chosen_all)
    return (hidden, jnp.stack(step_list, axis=0), owned_states)
```

```python
import functools

import jax
import jax.numpy as jnp
from jax import lax
from jax.experimental import pallas as pl
from jax.experimental.pallas import tpu as pltpu
from jax.sharding import PartitionSpec as P

S = 16
SEND_CAP = 2
EPSILON = 1e-05
LANES = 128
F32 = jnp.float32
BF16 = jnp.bfloat16
HIGH = lax.Precision.HIGHEST
VMEM_LIMIT = 48 * 1024 * 1024


def dot_nt(a, b, precision=None):
    return lax.dot_general(
        a, b, (((1,), (1,)), ((), ())), precision=precision, preferred_element_type=F32
    )


def dot_tn(a, b, precision=None):
    return lax.dot_general(
        a, b, (((0,), (0,)), ((), ())), precision=precision, preferred_element_type=F32
    )


def pick_kernel(count, slots, state_ref, *out_refs):
    for offset in range(count):
        for slot in range(SEND_CAP):
            request = slots[offset * SEND_CAP + slot]
            out_refs[offset][slot, 0] = state_ref[0, request].astype(BF16)


def pick_states(slot_requests, state_cache, count):
    layers, requests, heads, size, state = state_cache.shape
    out_block = pl.BlockSpec(
        (SEND_CAP, 1, heads, size, state), lambda layer, slots: (0, layer, 0, 0, 0)
    )
    return pl.pallas_call(
        functools.partial(pick_kernel, count),
        grid_spec=pltpu.PrefetchScalarGridSpec(
            num_scalar_prefetch=1,
            grid=(layers,),
            in_specs=[
                pl.BlockSpec(
                    (1, requests, heads, size, state), lambda layer, slots: (layer, 0, 0, 0, 0)
                )
            ],
            out_specs=[out_block] * count,
        ),
        out_shape=[jax.ShapeDtypeStruct((SEND_CAP, layers, heads, size, state), BF16)] * count,
        compiler_params=pltpu.CompilerParams(vmem_limit_bytes=VMEM_LIMIT),
        cost_estimate=pl.CostEstimate(
            flops=0, bytes_accessed=8 * 1024 * 1024, transcendentals=0
        ),
    )(slot_requests, state_cache)


def conv_silu(joined, prefix, incoming, kernel):
    taps = kernel.shape[0]
    length = incoming.shape[0]
    joined[8 - (taps - 1) : 8, :] = prefix
    joined[8 : 8 + length, :] = incoming
    first = 8 - (taps - 1)
    summed = joined[first : first + length, :] * kernel[0:1, :]
    for tap in range(1, taps):
        summed = summed + joined[first + tap : first + tap + length, :] * kernel[tap : tap + 1, :]
    return summed / (1.0 + jnp.exp(-summed))


def scan_kernel(
    model_width,
    slots,
    accepted,
    live,
    proj_ref,
    inner_cache,
    proj_cache,
    inner_kernel,
    proj_kernel,
    head_ref,
    state_ref,
    *rest,
):
    states_ref, gated_ref, weights_ref, b_ref, joined, joined_bc = rest[-6:]
    request = pl.program_id(0)
    heads, size, state = state_ref.shape[2:]
    inner = heads * size

    @pl.when(request == 0)
    def _():
        weights_ref[...] = jnp.zeros_like(weights_ref)

    block = proj_ref[...].astype(F32)
    tail = 2 * inner + 2 * state
    square = block[:, tail + heads : tail + heads + 1]
    scale = lax.rsqrt(square / model_width + EPSILON)
    gate = block[:, :inner] * scale
    x = conv_silu(
        joined, inner_cache[0, 0].astype(F32), block[:, inner : 2 * inner] * scale, inner_kernel[0]
    )
    bc = conv_silu(
        joined_bc, proj_cache[0, 0].astype(F32), block[:, 2 * inner : tail] * scale, proj_kernel[0]
    )
    b_val = bc[:, :state]
    c_val = bc[:, state:]
    b_half = b_val.astype(BF16)
    c_half = c_val.astype(BF16)
    raw = block[:, tail : tail + heads] * scale + head_ref[0, 0:1, :]
    delta = jnp.maximum(raw, 0.0) + jnp.log(1.0 + jnp.exp(-jnp.abs(raw)))
    log_decay = -delta * jnp.exp(head_ref[0, 1:2, :])
    decay = jnp.exp(log_decay)
    row = lax.broadcasted_iota(jnp.int32, (S, S), 0)
    column = lax.broadcasted_iota(jnp.int32, (S, S), 1)
    lower = (column <= row).astype(F32)
    cum_log = jnp.dot(lower, log_decay, precision=HIGH, preferred_element_type=F32)
    cum_log_t = dot_nt(
        (
            lax.broadcasted_iota(jnp.int32, (heads, heads), 0)
            == lax.broadcasted_iota(jnp.int32, (heads, heads), 1)
        ).astype(F32),
        cum_log,
        precision=HIGH,
    )
    taken = accepted[request]
    alive = live[request].astype(F32)
    steps = lax.broadcasted_iota(jnp.int32, (S, heads), 0)
    cum_end = jnp.sum(jnp.where(steps < taken, log_decay, 0.0), axis=0, keepdims=True)
    keep = jnp.where(steps < taken, jnp.exp(jnp.minimum(cum_end - cum_log, 0.0)), 0.0) * alive
    spread = (
        lax.broadcasted_iota(jnp.int32, (heads, inner), 1) // size
        == lax.broadcasted_iota(jnp.int32, (heads, inner), 0)
    ).astype(F32)
    stacked = jnp.concatenate([delta, jnp.exp(cum_log), keep], axis=0)
    wide = jnp.dot(stacked, spread, precision=HIGH, preferred_element_type=F32)
    skip_wide = jnp.dot(head_ref[0], spread, precision=HIGH, preferred_element_type=F32)[2:3]
    dx = wide[:S] * x
    dx_half = dx.astype(BF16)

    slot = slots[request]
    weights_ref[slot, :, :inner] = (wide[2 * S :] * dx).astype(BF16)
    end_row = jnp.broadcast_to(jnp.exp(cum_end) * alive, (S, heads))
    weights_ref[slot, :, inner:] = jnp.concatenate(
        [end_row, jnp.zeros((S, LANES - heads), F32)], axis=1
    ).astype(BF16)
    b_ref[0] = b_half

    start = state_ref[0, 0].reshape(inner, state)
    y = wide[S : 2 * S] * dot_nt(c_half, start.astype(BF16)) + skip_wide * x
    score = dot_nt(c_half, b_half)
    parts = []
    for head in range(heads):
        gap = jnp.minimum(cum_log[:, head : head + 1] - cum_log_t[head : head + 1, :], 0.0)
        weight = jnp.where(column <= row, jnp.exp(gap) * score, 0.0)
        parts.append(
            jnp.dot(
                weight.astype(BF16),
                dx_half[:, head * size : (head + 1) * size],
                preferred_element_type=F32,
            )
        )
    y = y + jnp.concatenate(parts, axis=1)
    gated_ref[...] = (y * (gate / (1.0 + jnp.exp(-gate)))).astype(BF16)

    dx_t = dx.T
    for head in range(heads):
        carried = state_ref[0, 0, head]
        for step in range(S):
            carried = (
                decay[step : step + 1, head : head + 1] * carried
                + dx_t[head * size : (head + 1) * size, step : step + 1] * b_val[step : step + 1, :]
            )
            states_ref[0, 0, step, head] = carried.astype(BF16)


def scan_layer(
    layer, model_width, count, slots, accepted, live, proj, inner_cache, proj_cache,
    inner_kernel, proj_kernel, head_rows, state_cache, states,
):
    layers, requests, heads, size, state = state_cache.shape
    inner = heads * size
    width = proj.shape[1]
    prefix = inner_cache.shape[2]
    taps = inner_kernel.shape[1]
    in_specs = [
        pl.BlockSpec((S, width), lambda q, *_: (q, 0)),
        pl.BlockSpec((1, 1, prefix, inner), lambda q, *_: (layer, q, 0, 0)),
        pl.BlockSpec((1, 1, prefix, 2 * state), lambda q, *_: (layer, q, 0, 0)),
        pl.BlockSpec((1, taps, inner), lambda q, *_: (layer, 0, 0)),
        pl.BlockSpec((1, taps, 2 * state), lambda q, *_: (layer, 0, 0)),
        pl.BlockSpec((1, 8, heads), lambda q, *_: (layer, 0, 0)),
        pl.BlockSpec((1, 1, heads, size, state), lambda q, *_: (layer, q, 0, 0, 0)),
    ]
    operands = [
        slots, accepted, live, proj, inner_cache, proj_cache, inner_kernel, proj_kernel,
        head_rows, state_cache,
    ]
    aliases = {}
    if states is not None:
        in_specs.append(pl.BlockSpec(memory_space=pl.ANY))
        aliases = {len(operands): 0}
        operands.append(states)
    return pl.pallas_call(
        functools.partial(scan_kernel, model_width),
        grid_spec=pltpu.PrefetchScalarGridSpec(
            num_scalar_prefetch=3,
            grid=(requests,),
            in_specs=in_specs,
            out_specs=[
                pl.BlockSpec((1, 1, S, heads, size, state), lambda q, *_: (layer, q, 0, 0, 0, 0)),
                pl.BlockSpec((S, inner), lambda q, *_: (q, 0)),
                pl.BlockSpec((count * SEND_CAP, S, inner + LANES), lambda q, *_: (0, 0, 0)),
                pl.BlockSpec((1, S, state), lambda q, *_: (q, 0, 0)),
            ],
            scratch_shapes=[
                pltpu.VMEM((8 + S, inner), F32),
                pltpu.VMEM((8 + S, 2 * state), F32),
            ],
        ),
        out_shape=[
            jax.ShapeDtypeStruct((layers, requests, S, heads, size, state), BF16),
            jax.ShapeDtypeStruct((requests * S, inner), BF16),
            jax.ShapeDtypeStruct((count * SEND_CAP, S, inner + LANES), BF16),
            jax.ShapeDtypeStruct((requests, S, state), BF16),
        ],
        input_output_aliases=aliases,
        compiler_params=pltpu.CompilerParams(vmem_limit_bytes=VMEM_LIMIT),
        cost_estimate=pl.CostEstimate(
            flops=requests * S * inner * state * 8,
            bytes_accessed=requests * S * inner * state * 3,
            transcendentals=0,
        ),
    )(*operands)


def owned_kernel(heads, size, mine, weights_ref, b_ref, *rest):
    start_refs, out_ref = rest[:-1], rest[-1]
    slot, layer = pl.program_id(0), pl.program_id(1)
    request = mine[slot]
    count = len(start_refs)
    column = lax.axis_index("col")
    inner = heads * size
    state = out_ref.shape[-1]
    b_half = b_ref[0, request]
    spread = (
        lax.broadcasted_iota(jnp.int32, (inner, heads), 0) // size
        == lax.broadcasted_iota(jnp.int32, (inner, heads), 1)
    ).astype(F32)
    for offset in range(count):
        source = lax.rem(column - offset + count, count)
        message = weights_ref[0, offset, 0]
        added = dot_tn(message[:, :inner], b_half)
        ends = message[0:1, inner : inner + heads].astype(F32)
        end = jnp.sum(spread * ends, axis=1, keepdims=True)
        start = start_refs[offset][0, 0].astype(F32).reshape(inner, state)
        out_ref[0, 0, 0, 0, pl.ds(source * heads, heads)] = (
            (end * start + added).astype(BF16).reshape(heads, size, state)
        )


def owned_states(mine, weights, b_all, starts, layers, heads, size, state):
    count = len(starts)
    requests = b_all.shape[1]
    width = weights.shape[-1]
    return pl.pallas_call(
        functools.partial(owned_kernel, heads, size),
        grid_spec=pltpu.PrefetchScalarGridSpec(
            num_scalar_prefetch=1,
            grid=(SEND_CAP, layers),
            in_specs=[
                pl.BlockSpec((1, count, 1, S, width), lambda r, l, *_: (l, 0, r, 0, 0)),
                pl.BlockSpec((1, requests, S, state), lambda r, l, *_: (l, 0, 0, 0)),
            ]
            + [pl.BlockSpec((1, 1, heads, size, state), lambda r, l, *_: (r, l, 0, 0, 0))] * count,
            out_specs=pl.BlockSpec(
                (1, 1, 1, 1, heads * count, size, state), lambda r, l, *_: (0, 0, r, l, 0, 0, 0)
            ),
        ),
        out_shape=jax.ShapeDtypeStruct(
            (1, 1, SEND_CAP, layers, heads * count, size, state), BF16
        ),
        compiler_params=pltpu.CompilerParams(vmem_limit_bytes=VMEM_LIMIT),
    )(mine, weights, b_all, *starts)


def rotate(array, offset, count):
    return lax.ppermute(array, "col", [(c, (c + offset) % count) for c in range(count)])


def local(
    hidden_states,
    input_gain,
    inner_weight,
    proj_weight,
    step_weight,
    inner_kernel,
    proj_kernel,
    step_bias,
    decay_log,
    skip_gain,
    norm_gain,
    out_weight,
    inner_cache,
    proj_cache,
    state_cache,
    accepted,
    owners,
    tenant_ranges,
):
    layers = inner_weight.shape[0]
    row_width = inner_weight.shape[1]
    inner = inner_weight.shape[3]
    heads = step_weight.shape[2]
    size = inner // heads
    state = proj_weight.shape[2] // 2
    requests = state_cache.shape[1]
    row_count = lax.axis_size("row")
    col_count = lax.axis_size("col")
    model_width = row_width * row_count
    inner_width = inner * col_count
    me = lax.axis_index("col")
    ids = jnp.arange(requests, dtype=jnp.int32)
    request_ids = lax.axis_index("row") * requests + ids
    live = jnp.any(
        (request_ids[:, None] >= tenant_ranges[None, :, 0])
        & (request_ids[:, None] < tenant_ranges[None, :, 1]),
        axis=1,
    ).astype(jnp.int32)
    earlier = (owners[:, None] == owners[None, :]) & (ids[None, :] < ids[:, None])
    ranks = jnp.sum(earlier.astype(jnp.int32), axis=1)
    slots = lax.rem(owners - me + col_count, col_count) * SEND_CAP + ranks
    grid = jnp.arange(col_count * SEND_CAP, dtype=jnp.int32)
    slot_requests = jnp.sum(
        jnp.where(slots[None, :] == grid[:, None], ids[None, :], 0), axis=1
    ).astype(jnp.int32)
    mine = slot_requests[:SEND_CAP]

    picked = pick_states(slot_requests, state_cache, col_count)
    starts = [picked[0]] + [
        rotate(picked[offset], offset, col_count) for offset in range(1, col_count)
    ]

    head_rows = jnp.pad(
        jnp.stack([step_bias, decay_log, skip_gain], axis=1), ((0, 0), (0, 5), (0, 0))
    )
    hidden = hidden_states
    states = None
    weight_layers = []
    b_layers = []
    for layer in range(layers):
        tokens = lax.all_gather(hidden, "col", axis=0, tiled=True).astype(F32)
        scaled = (tokens * input_gain[layer]).astype(BF16)
        square = jnp.sum(tokens * tokens, axis=1, keepdims=True)
        weight = inner_weight[layer].reshape(row_width, 2 * inner)
        partial = jnp.concatenate(
            [
                jnp.dot(scaled, weight, preferred_element_type=F32),
                jnp.dot(scaled, proj_weight[layer], preferred_element_type=F32),
                jnp.dot(scaled, step_weight[layer], preferred_element_type=F32),
                square,
                jnp.zeros((tokens.shape[0], LANES - heads - 1), F32),
            ],
            axis=1,
        )
        proj = lax.psum_scatter(partial, "row", scatter_dimension=0, tiled=True)
        states, gated, sent, b_half = scan_layer(
            layer, model_width, col_count, slots, accepted, live, proj, inner_cache, proj_cache,
            inner_kernel, proj_kernel, head_rows, state_cache, states,
        )
        weight_layers.append(sent)
        b_layers.append(b_half)
        gathered = lax.all_gather(gated, "row", axis=0, tiled=True).astype(F32)
        gate_square = jnp.sum(gathered * gathered, axis=1, keepdims=True)
        partial_out = jnp.dot(
            (gathered * norm_gain[layer]).astype(BF16),
            out_weight[layer],
            preferred_element_type=F32,
        )
        message = jnp.concatenate(
            [partial_out, jnp.broadcast_to(gate_square, (gathered.shape[0], LANES))], axis=1
        ).astype(BF16)
        total = lax.psum_scatter(message, "col", scatter_dimension=0, tiled=True).astype(F32)
        factor = lax.rsqrt(total[:, row_width : row_width + 1] / inner_width + EPSILON)
        hidden = (hidden.astype(F32) + total[:, :row_width] * factor).astype(BF16)

    sent = jnp.stack(weight_layers).reshape(layers, col_count, SEND_CAP, S, inner + LANES)
    received = [sent[:, 0]] + [
        rotate(sent[:, offset], offset, col_count) for offset in range(1, col_count)
    ]
    owned = owned_states(
        mine, jnp.stack(received, axis=1), jnp.stack(b_layers), starts, layers, heads, size, state
    )
    return (hidden, states, owned)


def solution(mesh):
    placed = (
        P("col", "row"),
        P(None, "row"),
        P(None, "row", None, "col"),
        P(None, "row", None),
        P(None, "row", "col"),
        P(None, None, "col"),
        P(),
        P(None, "col"),
        P(None, "col"),
        P(None, "col"),
        P(None, "col"),
        P(None, "col", "row"),
        P(None, "row", None, "col"),
        P(None, "row", None, None),
        P(None, "row", "col", None, None),
        P("row"),
        P("row"),
        P(),
    )
    return jax.shard_map(
        local,
        mesh=mesh,
        in_specs=placed,
        out_specs=(
            P("col", "row"),
            P(None, "row", None, "col", None, None),
            P("row", "col", None, None, None, None, None),
        ),
        check_vma=False,
    )
```

```python
import functools

import jax
import jax.numpy as jnp
from jax import lax
from jax.experimental import pallas as pl
from jax.experimental.pallas import tpu as pltpu
from jax.sharding import PartitionSpec as P

S = 16
SEND_CAP = 2
EPSILON = 1e-05
LANES = 128
F32 = jnp.float32
BF16 = jnp.bfloat16
HIGH = lax.Precision.HIGHEST
VMEM_LIMIT = 48 * 1024 * 1024
SMALL = pl.CostEstimate(flops=1000000, bytes_accessed=1000000, transcendentals=0)


def dot_nt(a, b, precision=None):
    return lax.dot_general(
        a, b, (((1,), (1,)), ((), ())), precision=precision, preferred_element_type=F32
    )


def dot_tn(a, b, precision=None):
    return lax.dot_general(
        a, b, (((0,), (0,)), ((), ())), precision=precision, preferred_element_type=F32
    )


def pick_kernel(count, slots, state_ref, *out_refs):
    for offset in range(count):
        for slot in range(SEND_CAP):
            request = slots[offset * SEND_CAP + slot]
            out_refs[offset][slot, 0] = state_ref[0, request].astype(BF16)


def pick_states(slot_requests, state_cache, count):
    layers, requests, heads, size, state = state_cache.shape
    out_block = pl.BlockSpec(
        (SEND_CAP, 1, heads, size, state), lambda layer, slots: (0, layer, 0, 0, 0)
    )
    return pl.pallas_call(
        functools.partial(pick_kernel, count),
        grid_spec=pltpu.PrefetchScalarGridSpec(
            num_scalar_prefetch=1,
            grid=(layers,),
            in_specs=[
                pl.BlockSpec(
                    (1, requests, heads, size, state), lambda layer, slots: (layer, 0, 0, 0, 0)
                )
            ],
            out_specs=[out_block] * count,
        ),
        out_shape=[jax.ShapeDtypeStruct((SEND_CAP, layers, heads, size, state), BF16)] * count,
        compiler_params=pltpu.CompilerParams(vmem_limit_bytes=VMEM_LIMIT),
        cost_estimate=pl.CostEstimate(
            flops=0, bytes_accessed=8 * 1024 * 1024, transcendentals=0
        ),
    )(slot_requests, state_cache)


def conv_silu(joined, prefix, incoming, kernel):
    taps = kernel.shape[0]
    length = incoming.shape[0]
    joined[8 - (taps - 1) : 8, :] = prefix
    joined[8 : 8 + length, :] = incoming
    first = 8 - (taps - 1)
    summed = joined[first : first + length, :] * kernel[0:1, :]
    for tap in range(1, taps):
        summed = summed + joined[first + tap : first + tap + length, :] * kernel[tap : tap + 1, :]
    return summed / (1.0 + jnp.exp(-summed))


def scan_kernel(
    model_width,
    slots,
    accepted,
    live,
    proj_ref,
    inner_cache,
    proj_cache,
    inner_kernel,
    proj_kernel,
    head_ref,
    state_ref,
    *rest,
):
    states_ref, gated_ref, weights_ref, b_ref, joined, joined_bc = rest[-6:]
    request = pl.program_id(0)
    heads, size, state = state_ref.shape[2:]
    inner = heads * size

    @pl.when(request == 0)
    def _():
        weights_ref[...] = jnp.zeros_like(weights_ref)

    block = proj_ref[...].astype(F32)
    tail = 2 * inner + 2 * state
    square = block[:, tail + heads : tail + heads + 1]
    scale = lax.rsqrt(square / model_width + EPSILON)
    gate = block[:, :inner] * scale
    x = conv_silu(
        joined, inner_cache[0, 0].astype(F32), block[:, inner : 2 * inner] * scale, inner_kernel[0]
    )
    bc = conv_silu(
        joined_bc, proj_cache[0, 0].astype(F32), block[:, 2 * inner : tail] * scale, proj_kernel[0]
    )
    b_val = bc[:, :state]
    c_val = bc[:, state:]
    b_half = b_val.astype(BF16)
    c_half = c_val.astype(BF16)
    raw = block[:, tail : tail + heads] * scale + head_ref[0, 0:1, :]
    delta = jnp.maximum(raw, 0.0) + jnp.log(1.0 + jnp.exp(-jnp.abs(raw)))
    log_decay = -delta * jnp.exp(head_ref[0, 1:2, :])
    decay = jnp.exp(log_decay)
    row = lax.broadcasted_iota(jnp.int32, (S, S), 0)
    column = lax.broadcasted_iota(jnp.int32, (S, S), 1)
    lower = (column <= row).astype(F32)
    cum_log = jnp.dot(lower, log_decay, precision=HIGH, preferred_element_type=F32)
    cum_log_t = dot_nt(
        (
            lax.broadcasted_iota(jnp.int32, (heads, heads), 0)
            == lax.broadcasted_iota(jnp.int32, (heads, heads), 1)
        ).astype(F32),
        cum_log,
        precision=HIGH,
    )
    taken = accepted[request]
    alive = live[request].astype(F32)
    steps = lax.broadcasted_iota(jnp.int32, (S, heads), 0)
    cum_end = jnp.sum(jnp.where(steps < taken, log_decay, 0.0), axis=0, keepdims=True)
    keep = jnp.where(steps < taken, jnp.exp(jnp.minimum(cum_end - cum_log, 0.0)), 0.0) * alive
    spread = (
        lax.broadcasted_iota(jnp.int32, (heads, inner), 1) // size
        == lax.broadcasted_iota(jnp.int32, (heads, inner), 0)
    ).astype(F32)
    stacked = jnp.concatenate([delta, jnp.exp(cum_log), keep], axis=0)
    wide = jnp.dot(stacked, spread, precision=HIGH, preferred_element_type=F32)
    skip_wide = jnp.dot(head_ref[0], spread, precision=HIGH, preferred_element_type=F32)[2:3]
    dx = wide[:S] * x
    dx_half = dx.astype(BF16)

    slot = slots[request]
    weights_ref[slot, :, :inner] = (wide[2 * S :] * dx).astype(BF16)
    end_row = jnp.broadcast_to(jnp.exp(cum_end) * alive, (S, heads))
    weights_ref[slot, :, inner:] = jnp.concatenate(
        [end_row, jnp.zeros((S, LANES - heads), F32)], axis=1
    ).astype(BF16)
    b_ref[0] = b_half

    start = state_ref[0, 0].reshape(inner, state)
    y = wide[S : 2 * S] * dot_nt(c_half, start.astype(BF16)) + skip_wide * x
    score = dot_nt(c_half, b_half)
    parts = []
    for head in range(heads):
        gap = jnp.minimum(cum_log[:, head : head + 1] - cum_log_t[head : head + 1, :], 0.0)
        weight = jnp.where(column <= row, jnp.exp(gap) * score, 0.0)
        parts.append(
            jnp.dot(
                weight.astype(BF16),
                dx_half[:, head * size : (head + 1) * size],
                preferred_element_type=F32,
            )
        )
    y = y + jnp.concatenate(parts, axis=1)
    gated_ref[...] = (y * (gate / (1.0 + jnp.exp(-gate)))).astype(BF16)

    dx_t = dx.T
    for head in range(heads):
        carried = state_ref[0, 0, head]
        for step in range(S):
            carried = (
                decay[step : step + 1, head : head + 1] * carried
                + dx_t[head * size : (head + 1) * size, step : step + 1] * b_val[step : step + 1, :]
            )
            states_ref[0, 0, step, head] = carried.astype(BF16)


def scan_layer(
    layer, model_width, count, slots, accepted, live, proj, inner_cache, proj_cache,
    inner_kernel, proj_kernel, head_rows, state_cache, states,
):
    layers, requests, heads, size, state = state_cache.shape
    inner = heads * size
    width = proj.shape[1]
    prefix = inner_cache.shape[2]
    taps = inner_kernel.shape[1]
    in_specs = [
        pl.BlockSpec((S, width), lambda q, *_: (q, 0)),
        pl.BlockSpec((1, 1, prefix, inner), lambda q, *_: (layer, q, 0, 0)),
        pl.BlockSpec((1, 1, prefix, 2 * state), lambda q, *_: (layer, q, 0, 0)),
        pl.BlockSpec((1, taps, inner), lambda q, *_: (layer, 0, 0)),
        pl.BlockSpec((1, taps, 2 * state), lambda q, *_: (layer, 0, 0)),
        pl.BlockSpec((1, 8, heads), lambda q, *_: (layer, 0, 0)),
        pl.BlockSpec((1, 1, heads, size, state), lambda q, *_: (layer, q, 0, 0, 0)),
    ]
    operands = [
        slots, accepted, live, proj, inner_cache, proj_cache, inner_kernel, proj_kernel,
        head_rows, state_cache,
    ]
    aliases = {}
    if states is not None:
        in_specs.append(pl.BlockSpec(memory_space=pl.ANY))
        aliases = {len(operands): 0}
        operands.append(states)
    return pl.pallas_call(
        functools.partial(scan_kernel, model_width),
        grid_spec=pltpu.PrefetchScalarGridSpec(
            num_scalar_prefetch=3,
            grid=(requests,),
            in_specs=in_specs,
            out_specs=[
                pl.BlockSpec((1, 1, S, heads, size, state), lambda q, *_: (layer, q, 0, 0, 0, 0)),
                pl.BlockSpec((S, inner), lambda q, *_: (q, 0)),
                pl.BlockSpec((count * SEND_CAP, S, inner + LANES), lambda q, *_: (0, 0, 0)),
                pl.BlockSpec((1, S, state), lambda q, *_: (q, 0, 0)),
            ],
            scratch_shapes=[
                pltpu.VMEM((8 + S, inner), F32),
                pltpu.VMEM((8 + S, 2 * state), F32),
            ],
        ),
        out_shape=[
            jax.ShapeDtypeStruct((layers, requests, S, heads, size, state), BF16),
            jax.ShapeDtypeStruct((requests * S, inner), BF16),
            jax.ShapeDtypeStruct((count * SEND_CAP, S, inner + LANES), BF16),
            jax.ShapeDtypeStruct((requests, S, state), BF16),
        ],
        input_output_aliases=aliases,
        compiler_params=pltpu.CompilerParams(vmem_limit_bytes=VMEM_LIMIT),
        cost_estimate=SMALL,
    )(*operands)


def owned_kernel(heads, size, mine, weights_ref, b_ref, *rest):
    start_refs, out_ref = rest[:-1], rest[-1]
    slot, layer = pl.program_id(0), pl.program_id(1)
    request = mine[slot]
    count = len(start_refs)
    column = lax.axis_index("col")
    inner = heads * size
    state = out_ref.shape[-1]
    b_half = b_ref[0, request]
    spread = (
        lax.broadcasted_iota(jnp.int32, (inner, heads), 0) // size
        == lax.broadcasted_iota(jnp.int32, (inner, heads), 1)
    ).astype(F32)
    for offset in range(count):
        source = lax.rem(column - offset + count, count)
        message = weights_ref[0, offset, 0]
        added = dot_tn(message[:, :inner], b_half)
        ends = message[0:1, inner : inner + heads].astype(F32)
        end = jnp.sum(spread * ends, axis=1, keepdims=True)
        start = start_refs[offset][0, 0].astype(F32).reshape(inner, state)
        out_ref[0, 0, 0, 0, pl.ds(source * heads, heads)] = (
            (end * start + added).astype(BF16).reshape(heads, size, state)
        )


def owned_states(mine, weights, b_all, starts, layers, heads, size, state):
    count = len(starts)
    requests = b_all.shape[1]
    width = weights.shape[-1]
    return pl.pallas_call(
        functools.partial(owned_kernel, heads, size),
        grid_spec=pltpu.PrefetchScalarGridSpec(
            num_scalar_prefetch=1,
            grid=(SEND_CAP, layers),
            in_specs=[
                pl.BlockSpec((1, count, 1, S, width), lambda r, l, *_: (l, 0, r, 0, 0)),
                pl.BlockSpec((1, requests, S, state), lambda r, l, *_: (l, 0, 0, 0)),
            ]
            + [pl.BlockSpec((1, 1, heads, size, state), lambda r, l, *_: (r, l, 0, 0, 0))] * count,
            out_specs=pl.BlockSpec(
                (1, 1, 1, 1, heads * count, size, state), lambda r, l, *_: (0, 0, r, l, 0, 0, 0)
            ),
        ),
        out_shape=jax.ShapeDtypeStruct(
            (1, 1, SEND_CAP, layers, heads * count, size, state), BF16
        ),
        compiler_params=pltpu.CompilerParams(vmem_limit_bytes=VMEM_LIMIT),
    )(mine, weights, b_all, *starts)


MESH = pl.DeviceIdType.MESH


def greet(count, row_count):
    column, row = lax.axis_index("col"), lax.axis_index("row")
    chips = row_count // 2
    chip, core = lax.div(row, 2), lax.rem(row, 2)
    barrier = pltpu.get_barrier_semaphore()
    for offset in range(1, count):
        pl.semaphore_signal(
            barrier, inc=1, device_id={"col": lax.rem(column + offset, count)}, device_id_type=MESH
        )
    pl.semaphore_signal(
        barrier, inc=1, device_id={"row": chip * 2 + 1 - core}, device_id_type=MESH
    )
    for step in range(1, chips):
        other = lax.rem(chip + step, chips) * 2 + core
        pl.semaphore_signal(barrier, inc=1, device_id={"row": other}, device_id_type=MESH)
    pl.semaphore_wait(barrier, count - 1 + 1 + chips - 1)
    return column, row, chips, chip, core


def push(source, target, send, receive, device):
    copy = pltpu.make_async_remote_copy(
        src_ref=source,
        dst_ref=target,
        send_sem=send,
        recv_sem=receive,
        device_id=device,
        device_id_type=MESH,
    )
    copy.start()
    return copy


def project_kernel(
    count, row_count, heads, hidden_ref, gain_ref, weight_ref, out_ref,
    blocks, kept, core_out, core_in, row_out, row_in,
    gather_send, gather_recv, core_send, core_recv, row_send, row_recv,
):
    column, row, chips, chip, core = greet(count, row_count)
    per_row = count // row_count
    tokens, depth = hidden_ref.shape
    width = weight_ref.shape[1]
    tail = width - LANES
    sends = []
    for offset in range(1, count):
        sends.append(
            push(
                hidden_ref, blocks.at[column], gather_send.at[offset], gather_recv.at[column],
                {"col": lax.rem(column + offset, count)},
            )
        )
    blocks[column] = hidden_ref[...]
    lane = lax.broadcasted_iota(jnp.int32, (per_row * tokens, LANES), 1)

    def partial(owner):
        for index in range(per_row):
            source = owner * per_row + index

            @pl.when(source != column)
            def _():
                pltpu.make_async_remote_copy(
                    src_ref=hidden_ref,
                    dst_ref=blocks.at[source],
                    send_sem=gather_send.at[0],
                    recv_sem=gather_recv.at[source],
                    device_id={"col": source},
                    device_id_type=MESH,
                ).wait_recv()

        block = blocks[pl.ds(owner * per_row, per_row)].reshape(per_row * tokens, depth)
        block = block.astype(F32)
        square = jnp.sum(block * block, axis=1, keepdims=True)
        product = jnp.dot(
            (block * gain_ref[...]).astype(BF16), weight_ref[...], preferred_element_type=F32
        )
        last = product[:, tail:] + jnp.where(lane == heads, square, 0.0)
        return product[:, :tail], last

    core_copies = []
    row_copies = []

    def forward(step):
        core_copies[step].wait_recv()
        kept[step] = kept[step] + core_in[step].astype(F32)
        if step < chips - 1:
            row_out[step] = kept[step].astype(BF16)
            row_copies.append(
                push(
                    row_out.at[step], row_in.at[step], row_send.at[step], row_recv.at[step],
                    {"row": lax.rem(chip + 1 + step, chips) * 2 + core},
                )
            )

    for step in range(chips):
        target = lax.rem(chip + 1 + step, chips)
        main, last = partial(target * 2 + 1 - core)
        core_out[step, :, :tail] = main.astype(BF16)
        core_out[step, :, tail:] = last.astype(BF16)
        core_copies.append(
            push(
                core_out.at[step], core_in.at[step], core_send.at[step], core_recv.at[step],
                {"row": chip * 2 + 1 - core},
            )
        )
        if step > 0:
            forward(step - 1)
        main, last = partial(target * 2 + core)
        kept[step, :, :tail] = main
        kept[step, :, tail:] = last
    forward(chips - 1)
    total = kept[chips - 1]
    for step in range(chips - 1):
        row_copies[step].wait_recv()
        total = total + row_in[step].astype(F32)
    out_ref[...] = total
    for copy in sends + core_copies + row_copies:
        copy.wait_send()


def project(layer, count, row_count, heads, hidden, gain, weight):
    tokens, depth = hidden.shape
    width = weight.shape[1]
    rows = tokens * (count // row_count)
    chips = row_count // 2
    vmem = pl.BlockSpec(memory_space=pltpu.VMEM)
    return pl.pallas_call(
        functools.partial(project_kernel, count, row_count, heads),
        out_shape=jax.ShapeDtypeStruct((rows, width), F32),
        in_specs=[vmem] * 3,
        out_specs=vmem,
        scratch_shapes=[
            pltpu.VMEM((count, tokens, depth), BF16),
            pltpu.VMEM((chips, rows, width), F32),
            pltpu.VMEM((chips, rows, width), BF16),
            pltpu.VMEM((chips, rows, width), BF16),
            pltpu.VMEM((chips, rows, width), BF16),
            pltpu.VMEM((chips, rows, width), BF16),
            pltpu.SemaphoreType.DMA((count,)),
            pltpu.SemaphoreType.DMA((count,)),
            pltpu.SemaphoreType.DMA((chips,)),
            pltpu.SemaphoreType.DMA((chips,)),
            pltpu.SemaphoreType.DMA((chips,)),
            pltpu.SemaphoreType.DMA((chips,)),
        ],
        compiler_params=pltpu.CompilerParams(
            collective_id=2 * layer, has_side_effects=True, vmem_limit_bytes=VMEM_LIMIT
        ),
        cost_estimate=SMALL,
    )(hidden, gain, weight)


def output_kernel(
    count, row_count, inner_width, gated_ref, gain_ref, weight_ref, hidden_ref, sent_ref,
    out_ref, received_ref,
    groups, outbox, inbox, taken,
    row_send, row_recv, relay_send, relay_recv, sum_send, sum_recv, state_send, state_recv,
):
    column, row, chips, chip, core = greet(count, row_count)
    per_row = count // row_count
    rows, inner = gated_ref.shape
    tokens, depth = hidden_ref.shape
    peer = {"row": chip * 2 + 1 - core}
    near = [push(gated_ref, groups.at[1], row_send.at[0], row_recv.at[0], peer)]
    for step in range(1, chips):
        near.append(
            push(
                gated_ref, groups.at[2 * step], row_send.at[step], row_recv.at[step],
                {"row": lax.rem(chip - step + chips, chips) * 2 + core},
            )
        )
    state_copies = []

    def process(group, owner):
        value = group.astype(F32)
        square = jnp.sum(value * value, axis=1, keepdims=True)
        product = jnp.dot(
            (value * gain_ref[...]).astype(BF16), weight_ref[...], preferred_element_type=F32
        )
        product = product.astype(BF16).reshape(per_row, tokens, depth)
        square = jnp.broadcast_to(square, (rows, LANES)).astype(BF16)
        square = square.reshape(per_row, tokens, LANES)
        for index in range(per_row):
            target = owner * per_row + index
            outbox[target, :, :depth] = product[index]
            outbox[target, :, depth:] = square[index]

            @pl.when(target != column)
            def _():
                push(
                    outbox.at[target], inbox.at[column], sum_send.at[target], sum_recv.at[column],
                    {"col": target},
                )

    process(gated_ref[...], row)
    near[0].wait_recv()
    process(groups[1], chip * 2 + 1 - core)
    relays = []
    for step in range(1, chips):
        near[step].wait_recv()
        relays.append(
            push(
                groups.at[2 * step], groups.at[2 * step + 1], relay_send.at[step],
                relay_recv.at[step], peer,
            )
        )
        process(groups[2 * step], lax.rem(chip + step, chips) * 2 + core)
    for step in range(1, chips):
        relays[step - 1].wait_recv()
        process(groups[2 * step + 1], lax.rem(chip + step, chips) * 2 + 1 - core)
    for offset in range(1, count):
        state_copies.append(
            push(
                sent_ref.at[offset], taken.at[offset], state_send.at[offset],
                state_recv.at[offset], {"col": lax.rem(column + offset, count)},
            )
        )
    received_ref[0] = sent_ref[0]
    total = outbox[column].astype(F32)
    for offset in range(1, count):
        source = lax.rem(column + offset, count)
        arrival = pltpu.make_async_remote_copy(
            src_ref=outbox.at[source],
            dst_ref=inbox.at[source],
            send_sem=sum_send.at[source],
            recv_sem=sum_recv.at[source],
            device_id={"col": source},
            device_id_type=MESH,
        )
        arrival.wait_recv()
        total = total + inbox[source].astype(F32)
        arrival.wait_send()
    factor = lax.rsqrt(total[:, depth : depth + 1] / inner_width + EPSILON)
    out_ref[...] = (hidden_ref[...].astype(F32) + total[:, :depth] * factor).astype(BF16)
    for offset in range(1, count):
        state_copies[offset - 1].wait()
        received_ref[offset] = taken[offset]
    for copy in near + relays:
        copy.wait_send()


def output(layer, count, row_count, inner_width, gated, gain, weight, hidden, sent):
    tokens, depth = hidden.shape
    rows, inner = gated.shape
    chips = row_count // 2
    vmem = pl.BlockSpec(memory_space=pltpu.VMEM)
    dma = pltpu.SemaphoreType.DMA
    return pl.pallas_call(
        functools.partial(output_kernel, count, row_count, inner_width),
        out_shape=[
            jax.ShapeDtypeStruct((tokens, depth), BF16),
            jax.ShapeDtypeStruct(sent.shape, BF16),
        ],
        in_specs=[vmem] * 5,
        out_specs=[vmem] * 2,
        scratch_shapes=[
            pltpu.VMEM((row_count, rows, inner), BF16),
            pltpu.VMEM((count, tokens, depth + LANES), BF16),
            pltpu.VMEM((count, tokens, depth + LANES), BF16),
            pltpu.VMEM(sent.shape, BF16),
            dma((chips,)),
            dma((chips,)),
            dma((chips,)),
            dma((chips,)),
            dma((count,)),
            dma((count,)),
            dma((count,)),
            dma((count,)),
        ],
        compiler_params=pltpu.CompilerParams(
            collective_id=2 * layer + 1, has_side_effects=True, vmem_limit_bytes=VMEM_LIMIT
        ),
        cost_estimate=SMALL,
    )(gated, gain, weight, hidden, sent)


def rotate(array, offset, count):
    return lax.ppermute(array, "col", [(c, (c + offset) % count) for c in range(count)])


def local(
    hidden_states,
    input_gain,
    inner_weight,
    proj_weight,
    step_weight,
    inner_kernel,
    proj_kernel,
    step_bias,
    decay_log,
    skip_gain,
    norm_gain,
    out_weight,
    inner_cache,
    proj_cache,
    state_cache,
    accepted,
    owners,
    tenant_ranges,
):
    layers = inner_weight.shape[0]
    row_width = inner_weight.shape[1]
    inner = inner_weight.shape[3]
    heads = step_weight.shape[2]
    size = inner // heads
    state = proj_weight.shape[2] // 2
    requests = state_cache.shape[1]
    row_count = lax.axis_size("row")
    col_count = lax.axis_size("col")
    model_width = row_width * row_count
    inner_width = inner * col_count
    me = lax.axis_index("col")
    ids = jnp.arange(requests, dtype=jnp.int32)
    request_ids = lax.axis_index("row") * requests + ids
    live = jnp.any(
        (request_ids[:, None] >= tenant_ranges[None, :, 0])
        & (request_ids[:, None] < tenant_ranges[None, :, 1]),
        axis=1,
    ).astype(jnp.int32)
    earlier = (owners[:, None] == owners[None, :]) & (ids[None, :] < ids[:, None])
    ranks = jnp.sum(earlier.astype(jnp.int32), axis=1)
    slots = lax.rem(owners - me + col_count, col_count) * SEND_CAP + ranks
    grid = jnp.arange(col_count * SEND_CAP, dtype=jnp.int32)
    slot_requests = jnp.sum(
        jnp.where(slots[None, :] == grid[:, None], ids[None, :], 0), axis=1
    ).astype(jnp.int32)
    mine = slot_requests[:SEND_CAP]

    picked = pick_states(slot_requests, state_cache, col_count)
    hidden, picked = lax.optimization_barrier((hidden_states, picked))
    starts = [picked[0]] + [
        rotate(picked[offset], offset, col_count) for offset in range(1, col_count)
    ]

    head_rows = jnp.pad(
        jnp.stack([step_bias, decay_log, skip_gain], axis=1), ((0, 0), (0, 5), (0, 0))
    )
    states = None
    weight_layers = []
    b_layers = []
    for layer in range(layers):
        weight = jnp.concatenate(
            [
                inner_weight[layer].reshape(row_width, 2 * inner),
                proj_weight[layer],
                step_weight[layer],
                jnp.zeros((row_width, LANES - heads), BF16),
            ],
            axis=1,
        )
        proj = project(
            layer, col_count, row_count, heads, hidden, input_gain[layer : layer + 1], weight
        )
        states, gated, sent, b_half = scan_layer(
            layer, model_width, col_count, slots, accepted, live, proj, inner_cache, proj_cache,
            inner_kernel, proj_kernel, head_rows, state_cache, states,
        )
        b_layers.append(b_half)
        if layer == layers - 1:
            gated, starts = lax.optimization_barrier((gated, starts))
        hidden, received = output(
            layer, col_count, row_count, inner_width, gated, norm_gain[layer : layer + 1],
            out_weight[layer], hidden,
            sent.reshape(col_count, SEND_CAP, S, inner + LANES),
        )
        weight_layers.append(received)
    owned = owned_states(
        mine, jnp.stack(weight_layers), jnp.stack(b_layers), starts, layers, heads, size, state
    )
    return (hidden, states, owned)


def solution(mesh):
    placed = (
        P("col", "row"),
        P(None, "row"),
        P(None, "row", None, "col"),
        P(None, "row", None),
        P(None, "row", "col"),
        P(None, None, "col"),
        P(),
        P(None, "col"),
        P(None, "col"),
        P(None, "col"),
        P(None, "col"),
        P(None, "col", "row"),
        P(None, "row", None, "col"),
        P(None, "row", None, None),
        P(None, "row", "col", None, None),
        P("row"),
        P("row"),
        P(),
    )
    return jax.shard_map(
        local,
        mesh=mesh,
        in_specs=placed,
        out_specs=(
            P("col", "row"),
            P(None, "row", None, "col", None, None),
            P("row", "col", None, None, None, None, None),
        ),
        check_vma=False,
    )
```

```python
import functools

import jax
import jax.numpy as jnp
from jax import lax
from jax.experimental import pallas as pl
from jax.experimental.pallas import tpu as pltpu
from jax.sharding import PartitionSpec as P

S = 16
SEND_CAP = 2
EPSILON = 1e-05
LANES = 128
F32 = jnp.float32
BF16 = jnp.bfloat16
HIGH = lax.Precision.HIGHEST
VMEM_LIMIT = 48 * 1024 * 1024
SMALL = pl.CostEstimate(flops=1000000, bytes_accessed=1000000, transcendentals=0)


def dot_nt(a, b, precision=None):
    return lax.dot_general(
        a, b, (((1,), (1,)), ((), ())), precision=precision, preferred_element_type=F32
    )


def dot_tn(a, b, precision=None):
    return lax.dot_general(
        a, b, (((0,), (0,)), ((), ())), precision=precision, preferred_element_type=F32
    )


def pick_kernel(count, slots, state_ref, *out_refs):
    for offset in range(count):
        for slot in range(SEND_CAP):
            request = slots[offset * SEND_CAP + slot]
            out_refs[offset][slot, 0] = state_ref[0, request].astype(BF16)


def pick_states(slot_requests, state_cache, count):
    layers, requests, heads, size, state = state_cache.shape
    out_block = pl.BlockSpec(
        (SEND_CAP, 1, heads, size, state), lambda layer, slots: (0, layer, 0, 0, 0)
    )
    return pl.pallas_call(
        functools.partial(pick_kernel, count),
        grid_spec=pltpu.PrefetchScalarGridSpec(
            num_scalar_prefetch=1,
            grid=(layers,),
            in_specs=[
                pl.BlockSpec(
                    (1, requests, heads, size, state), lambda layer, slots: (layer, 0, 0, 0, 0)
                )
            ],
            out_specs=[out_block] * count,
        ),
        out_shape=[jax.ShapeDtypeStruct((SEND_CAP, layers, heads, size, state), BF16)] * count,
        compiler_params=pltpu.CompilerParams(vmem_limit_bytes=VMEM_LIMIT),
        cost_estimate=pl.CostEstimate(
            flops=0, bytes_accessed=8 * 1024 * 1024, transcendentals=0
        ),
    )(slot_requests, state_cache)


def conv_silu(joined, prefix, incoming, kernel):
    taps = kernel.shape[0]
    length = incoming.shape[0]
    joined[8 - (taps - 1) : 8, :] = prefix
    joined[8 : 8 + length, :] = incoming
    first = 8 - (taps - 1)
    summed = joined[first : first + length, :] * kernel[0:1, :]
    for tap in range(1, taps):
        summed = summed + joined[first + tap : first + tap + length, :] * kernel[tap : tap + 1, :]
    return summed / (1.0 + jnp.exp(-summed))


def scan_kernel(
    model_width,
    slots,
    accepted,
    live,
    proj_ref,
    inner_cache,
    proj_cache,
    inner_kernel,
    proj_kernel,
    head_ref,
    state_ref,
    *rest,
):
    states_ref, gated_ref, weights_ref, b_ref, joined, joined_bc = rest[-6:]
    request = pl.program_id(0)
    heads, size, state = state_ref.shape[2:]
    inner = heads * size

    @pl.when(request == 0)
    def _():
        weights_ref[...] = jnp.zeros_like(weights_ref)

    block = proj_ref[...].astype(F32)
    tail = 2 * inner + 2 * state
    square = block[:, tail + heads : tail + heads + 1]
    scale = lax.rsqrt(square / model_width + EPSILON)
    gate = block[:, :inner] * scale
    x = conv_silu(
        joined, inner_cache[0, 0].astype(F32), block[:, inner : 2 * inner] * scale, inner_kernel[0]
    )
    bc = conv_silu(
        joined_bc, proj_cache[0, 0].astype(F32), block[:, 2 * inner : tail] * scale, proj_kernel[0]
    )
    b_val = bc[:, :state]
    c_val = bc[:, state:]
    b_half = b_val.astype(BF16)
    c_half = c_val.astype(BF16)
    raw = block[:, tail : tail + heads] * scale + head_ref[0, 0:1, :]
    delta = jnp.maximum(raw, 0.0) + jnp.log(1.0 + jnp.exp(-jnp.abs(raw)))
    log_decay = -delta * jnp.exp(head_ref[0, 1:2, :])
    decay = jnp.exp(log_decay)
    row = lax.broadcasted_iota(jnp.int32, (S, S), 0)
    column = lax.broadcasted_iota(jnp.int32, (S, S), 1)
    lower = (column <= row).astype(F32)
    cum_log = jnp.dot(lower, log_decay, precision=HIGH, preferred_element_type=F32)
    cum_log_t = dot_nt(
        (
            lax.broadcasted_iota(jnp.int32, (heads, heads), 0)
            == lax.broadcasted_iota(jnp.int32, (heads, heads), 1)
        ).astype(F32),
        cum_log,
        precision=HIGH,
    )
    taken = accepted[request]
    alive = live[request].astype(F32)
    steps = lax.broadcasted_iota(jnp.int32, (S, heads), 0)
    cum_end = jnp.sum(jnp.where(steps < taken, log_decay, 0.0), axis=0, keepdims=True)
    keep = jnp.where(steps < taken, jnp.exp(jnp.minimum(cum_end - cum_log, 0.0)), 0.0) * alive
    spread = (
        lax.broadcasted_iota(jnp.int32, (heads, inner), 1) // size
        == lax.broadcasted_iota(jnp.int32, (heads, inner), 0)
    ).astype(F32)
    stacked = jnp.concatenate([delta, jnp.exp(cum_log), keep], axis=0)
    wide = jnp.dot(stacked, spread, precision=HIGH, preferred_element_type=F32)
    skip_wide = jnp.dot(head_ref[0], spread, precision=HIGH, preferred_element_type=F32)[2:3]
    dx = wide[:S] * x
    dx_half = dx.astype(BF16)

    slot = slots[request]
    weights_ref[slot, :, :inner] = (wide[2 * S :] * dx).astype(BF16)
    end_row = jnp.broadcast_to(jnp.exp(cum_end) * alive, (S, heads))
    weights_ref[slot, :, inner:] = jnp.concatenate(
        [end_row, jnp.zeros((S, LANES - heads), F32)], axis=1
    ).astype(BF16)
    b_ref[0] = b_half

    start = state_ref[0, 0].reshape(inner, state)
    y = wide[S : 2 * S] * dot_nt(c_half, start.astype(BF16)) + skip_wide * x
    score = dot_nt(c_half, b_half)
    parts = []
    for head in range(heads):
        gap = jnp.minimum(cum_log[:, head : head + 1] - cum_log_t[head : head + 1, :], 0.0)
        weight = jnp.where(column <= row, jnp.exp(gap) * score, 0.0)
        parts.append(
            jnp.dot(
                weight.astype(BF16),
                dx_half[:, head * size : (head + 1) * size],
                preferred_element_type=F32,
            )
        )
    y = y + jnp.concatenate(parts, axis=1)
    gated_ref[...] = (y * (gate / (1.0 + jnp.exp(-gate)))).astype(BF16)

    dx_t = dx.T
    for head in range(heads):
        carried = state_ref[0, 0, head]
        for step in range(S):
            carried = (
                decay[step : step + 1, head : head + 1] * carried
                + dx_t[head * size : (head + 1) * size, step : step + 1] * b_val[step : step + 1, :]
            )
            states_ref[0, 0, step, head] = carried.astype(BF16)


def scan_layer(
    layer, model_width, count, slots, accepted, live, proj, inner_cache, proj_cache,
    inner_kernel, proj_kernel, head_rows, state_cache, states,
):
    layers, requests, heads, size, state = state_cache.shape
    inner = heads * size
    width = proj.shape[1]
    prefix = inner_cache.shape[2]
    taps = inner_kernel.shape[1]
    in_specs = [
        pl.BlockSpec((S, width), lambda q, *_: (q, 0)),
        pl.BlockSpec((1, 1, prefix, inner), lambda q, *_: (layer, q, 0, 0)),
        pl.BlockSpec((1, 1, prefix, 2 * state), lambda q, *_: (layer, q, 0, 0)),
        pl.BlockSpec((1, taps, inner), lambda q, *_: (layer, 0, 0)),
        pl.BlockSpec((1, taps, 2 * state), lambda q, *_: (layer, 0, 0)),
        pl.BlockSpec((1, 8, heads), lambda q, *_: (layer, 0, 0)),
        pl.BlockSpec((1, 1, heads, size, state), lambda q, *_: (layer, q, 0, 0, 0)),
    ]
    operands = [
        slots, accepted, live, proj, inner_cache, proj_cache, inner_kernel, proj_kernel,
        head_rows, state_cache,
    ]
    aliases = {}
    if states is not None:
        in_specs.append(pl.BlockSpec(memory_space=pl.ANY))
        aliases = {len(operands): 0}
        operands.append(states)
    return pl.pallas_call(
        functools.partial(scan_kernel, model_width),
        grid_spec=pltpu.PrefetchScalarGridSpec(
            num_scalar_prefetch=3,
            grid=(requests,),
            in_specs=in_specs,
            out_specs=[
                pl.BlockSpec((1, 1, S, heads, size, state), lambda q, *_: (layer, q, 0, 0, 0, 0)),
                pl.BlockSpec((S, inner), lambda q, *_: (q, 0)),
                pl.BlockSpec((count * SEND_CAP, S, inner + LANES), lambda q, *_: (0, 0, 0)),
                pl.BlockSpec((1, S, state), lambda q, *_: (q, 0, 0)),
            ],
            scratch_shapes=[
                pltpu.VMEM((8 + S, inner), F32),
                pltpu.VMEM((8 + S, 2 * state), F32),
            ],
        ),
        out_shape=[
            jax.ShapeDtypeStruct((layers, requests, S, heads, size, state), BF16),
            jax.ShapeDtypeStruct((requests * S, inner), BF16),
            jax.ShapeDtypeStruct((count * SEND_CAP, S, inner + LANES), BF16),
            jax.ShapeDtypeStruct((requests, S, state), BF16),
        ],
        input_output_aliases=aliases,
        compiler_params=pltpu.CompilerParams(vmem_limit_bytes=VMEM_LIMIT),
        cost_estimate=SMALL,
    )(*operands)


def owned_kernel(heads, size, mine, weights_ref, b_ref, *rest):
    start_refs, out_ref = rest[:-1], rest[-1]
    slot, layer = pl.program_id(0), pl.program_id(1)
    request = mine[slot]
    count = len(start_refs)
    column = lax.axis_index("col")
    inner = heads * size
    state = out_ref.shape[-1]
    b_half = b_ref[0, request]
    spread = (
        lax.broadcasted_iota(jnp.int32, (inner, heads), 0) // size
        == lax.broadcasted_iota(jnp.int32, (inner, heads), 1)
    ).astype(F32)
    for offset in range(count):
        source = lax.rem(column - offset + count, count)
        message = weights_ref[0, offset, 0]
        added = dot_tn(message[:, :inner], b_half)
        ends = message[0:1, inner : inner + heads].astype(F32)
        end = jnp.sum(spread * ends, axis=1, keepdims=True)
        start = start_refs[offset][0, 0].astype(F32).reshape(inner, state)
        out_ref[0, 0, 0, 0, pl.ds(source * heads, heads)] = (
            (end * start + added).astype(BF16).reshape(heads, size, state)
        )


def owned_states(mine, weights, b_all, starts, layers, heads, size, state):
    count = len(starts)
    requests = b_all.shape[1]
    width = weights.shape[-1]
    return pl.pallas_call(
        functools.partial(owned_kernel, heads, size),
        grid_spec=pltpu.PrefetchScalarGridSpec(
            num_scalar_prefetch=1,
            grid=(SEND_CAP, layers),
            in_specs=[
                pl.BlockSpec((1, count, 1, S, width), lambda r, l, *_: (l, 0, r, 0, 0)),
                pl.BlockSpec((1, requests, S, state), lambda r, l, *_: (l, 0, 0, 0)),
            ]
            + [pl.BlockSpec((1, 1, heads, size, state), lambda r, l, *_: (r, l, 0, 0, 0))] * count,
            out_specs=pl.BlockSpec(
                (1, 1, 1, 1, heads * count, size, state), lambda r, l, *_: (0, 0, r, l, 0, 0, 0)
            ),
        ),
        out_shape=jax.ShapeDtypeStruct(
            (1, 1, SEND_CAP, layers, heads * count, size, state), BF16
        ),
        compiler_params=pltpu.CompilerParams(vmem_limit_bytes=VMEM_LIMIT),
    )(mine, weights, b_all, *starts)


MESH = pl.DeviceIdType.MESH


def greet(count, row_count):
    column, row = lax.axis_index("col"), lax.axis_index("row")
    chips = row_count // 2
    chip, core = lax.div(row, 2), lax.rem(row, 2)
    barrier = pltpu.get_barrier_semaphore()
    for offset in range(1, count):
        pl.semaphore_signal(
            barrier, inc=1, device_id={"col": lax.rem(column + offset, count)}, device_id_type=MESH
        )
    pl.semaphore_signal(
        barrier, inc=1, device_id={"row": chip * 2 + 1 - core}, device_id_type=MESH
    )
    for step in range(1, chips):
        other = lax.rem(chip + step, chips) * 2 + core
        pl.semaphore_signal(barrier, inc=1, device_id={"row": other}, device_id_type=MESH)
    pl.semaphore_wait(barrier, count - 1 + 1 + chips - 1)
    return column, row, chips, chip, core


def push(source, target, send, receive, device):
    copy = pltpu.make_async_remote_copy(
        src_ref=source,
        dst_ref=target,
        send_sem=send,
        recv_sem=receive,
        device_id=device,
        device_id_type=MESH,
    )
    copy.start()
    return copy


def project_kernel(
    count, row_count, heads, hidden_ref, gain_ref, weight_ref, out_ref,
    blocks, kept, core_out, core_in, row_out, row_in,
    gather_send, gather_recv, core_send, core_recv, row_send, row_recv,
):
    column, row, chips, chip, core = greet(count, row_count)
    per_row = count // row_count
    tokens, depth = hidden_ref.shape
    width = weight_ref.shape[1]
    tail = width - LANES
    sends = []
    for offset in range(1, count):
        sends.append(
            push(
                hidden_ref, blocks.at[column], gather_send.at[offset], gather_recv.at[column],
                {"col": lax.rem(column + offset, count)},
            )
        )
    blocks[column] = hidden_ref[...]
    lane = lax.broadcasted_iota(jnp.int32, (per_row * tokens, LANES), 1)

    def partial(owner):
        for index in range(per_row):
            source = owner * per_row + index

            @pl.when(source != column)
            def _():
                pltpu.make_async_remote_copy(
                    src_ref=hidden_ref,
                    dst_ref=blocks.at[source],
                    send_sem=gather_send.at[0],
                    recv_sem=gather_recv.at[source],
                    device_id={"col": source},
                    device_id_type=MESH,
                ).wait_recv()

        block = blocks[pl.ds(owner * per_row, per_row)].reshape(per_row * tokens, depth)
        block = block.astype(F32)
        square = jnp.sum(block * block, axis=1, keepdims=True)
        product = jnp.dot(
            (block * gain_ref[...]).astype(BF16), weight_ref[...], preferred_element_type=F32
        )
        last = product[:, tail:] + jnp.where(lane == heads, square, 0.0)
        return product[:, :tail], last

    core_copies = []
    row_copies = []

    def forward(step):
        core_copies[step].wait_recv()
        kept[step] = kept[step] + core_in[step].astype(F32)
        if step < chips - 1:
            row_out[step] = kept[step].astype(BF16)
            row_copies.append(
                push(
                    row_out.at[step], row_in.at[step], row_send.at[step], row_recv.at[step],
                    {"row": lax.rem(chip + 1 + step, chips) * 2 + core},
                )
            )

    for step in range(chips):
        target = lax.rem(chip + 1 + step, chips)
        main, last = partial(target * 2 + 1 - core)
        core_out[step, :, :tail] = main.astype(BF16)
        core_out[step, :, tail:] = last.astype(BF16)
        core_copies.append(
            push(
                core_out.at[step], core_in.at[step], core_send.at[step], core_recv.at[step],
                {"row": chip * 2 + 1 - core},
            )
        )
        if step > 0:
            forward(step - 1)
        main, last = partial(target * 2 + core)
        kept[step, :, :tail] = main
        kept[step, :, tail:] = last
    forward(chips - 1)
    total = kept[chips - 1]
    for step in range(chips - 1):
        row_copies[step].wait_recv()
        total = total + row_in[step].astype(F32)
    out_ref[...] = total
    for copy in sends + core_copies + row_copies:
        copy.wait_send()


def project(layer, count, row_count, heads, hidden, gain, weight):
    tokens, depth = hidden.shape
    width = weight.shape[1]
    rows = tokens * (count // row_count)
    chips = row_count // 2
    vmem = pl.BlockSpec(memory_space=pltpu.VMEM)
    return pl.pallas_call(
        functools.partial(project_kernel, count, row_count, heads),
        out_shape=jax.ShapeDtypeStruct((rows, width), F32),
        in_specs=[vmem] * 3,
        out_specs=vmem,
        scratch_shapes=[
            pltpu.VMEM((count, tokens, depth), BF16),
            pltpu.VMEM((chips, rows, width), F32),
            pltpu.VMEM((chips, rows, width), BF16),
            pltpu.VMEM((chips, rows, width), BF16),
            pltpu.VMEM((chips, rows, width), BF16),
            pltpu.VMEM((chips, rows, width), BF16),
            pltpu.SemaphoreType.DMA((count,)),
            pltpu.SemaphoreType.DMA((count,)),
            pltpu.SemaphoreType.DMA((chips,)),
            pltpu.SemaphoreType.DMA((chips,)),
            pltpu.SemaphoreType.DMA((chips,)),
            pltpu.SemaphoreType.DMA((chips,)),
        ],
        compiler_params=pltpu.CompilerParams(
            collective_id=2 * layer, has_side_effects=True, vmem_limit_bytes=VMEM_LIMIT
        ),
        cost_estimate=SMALL,
    )(hidden, gain, weight)


def output_kernel(
    count, row_count, inner_width, gated_ref, gain_ref, weight_ref, hidden_ref, sent_ref,
    out_ref, received_ref,
    groups, outbox, inbox, taken,
    row_send, row_recv, relay_send, relay_recv, sum_send, sum_recv, state_send, state_recv,
):
    column, row, chips, chip, core = greet(count, row_count)
    per_row = count // row_count
    rows, inner = gated_ref.shape
    tokens, depth = hidden_ref.shape
    peer = {"row": chip * 2 + 1 - core}
    near = [push(gated_ref, groups.at[1], row_send.at[0], row_recv.at[0], peer)]
    for step in range(1, chips):
        near.append(
            push(
                gated_ref, groups.at[2 * step], row_send.at[step], row_recv.at[step],
                {"row": lax.rem(chip - step + chips, chips) * 2 + core},
            )
        )
    state_copies = []
    for offset in range(1, count):
        state_copies.append(
            push(
                sent_ref.at[offset], taken.at[offset], state_send.at[offset],
                state_recv.at[offset], {"col": lax.rem(column + offset, count)},
            )
        )

    def process(group, owner):
        value = group.astype(F32)
        square = jnp.sum(value * value, axis=1, keepdims=True)
        product = jnp.dot(
            (value * gain_ref[...]).astype(BF16), weight_ref[...], preferred_element_type=F32
        )
        product = product.astype(BF16).reshape(per_row, tokens, depth)
        square = jnp.broadcast_to(square, (rows, LANES)).astype(BF16)
        square = square.reshape(per_row, tokens, LANES)
        for index in range(per_row):
            target = owner * per_row + index
            outbox[target, :, :depth] = product[index]
            outbox[target, :, depth:] = square[index]

            @pl.when(target != column)
            def _():
                push(
                    outbox.at[target], inbox.at[column], sum_send.at[target], sum_recv.at[column],
                    {"col": target},
                )

    process(gated_ref[...], row)
    near[0].wait_recv()
    process(groups[1], chip * 2 + 1 - core)
    relays = []
    for step in range(1, chips):
        near[step].wait_recv()
        relays.append(
            push(
                groups.at[2 * step], groups.at[2 * step + 1], relay_send.at[step],
                relay_recv.at[step], peer,
            )
        )
        process(groups[2 * step], lax.rem(chip + step, chips) * 2 + core)
    for step in range(1, chips):
        relays[step - 1].wait_recv()
        process(groups[2 * step + 1], lax.rem(chip + step, chips) * 2 + 1 - core)
    received_ref[0] = sent_ref[0]
    total = outbox[column].astype(F32)
    for offset in range(1, count):
        source = lax.rem(column + offset, count)
        arrival = pltpu.make_async_remote_copy(
            src_ref=outbox.at[source],
            dst_ref=inbox.at[source],
            send_sem=sum_send.at[source],
            recv_sem=sum_recv.at[source],
            device_id={"col": source},
            device_id_type=MESH,
        )
        arrival.wait_recv()
        total = total + inbox[source].astype(F32)
        arrival.wait_send()
    factor = lax.rsqrt(total[:, depth : depth + 1] / inner_width + EPSILON)
    out_ref[...] = (hidden_ref[...].astype(F32) + total[:, :depth] * factor).astype(BF16)
    for offset in range(1, count):
        state_copies[offset - 1].wait()
        received_ref[offset] = taken[offset]
    for copy in near + relays:
        copy.wait_send()


def output(layer, count, row_count, inner_width, gated, gain, weight, hidden, sent):
    tokens, depth = hidden.shape
    rows, inner = gated.shape
    chips = row_count // 2
    vmem = pl.BlockSpec(memory_space=pltpu.VMEM)
    dma = pltpu.SemaphoreType.DMA
    return pl.pallas_call(
        functools.partial(output_kernel, count, row_count, inner_width),
        out_shape=[
            jax.ShapeDtypeStruct((tokens, depth), BF16),
            jax.ShapeDtypeStruct(sent.shape, BF16),
        ],
        in_specs=[vmem] * 5,
        out_specs=[vmem] * 2,
        scratch_shapes=[
            pltpu.VMEM((row_count, rows, inner), BF16),
            pltpu.VMEM((count, tokens, depth + LANES), BF16),
            pltpu.VMEM((count, tokens, depth + LANES), BF16),
            pltpu.VMEM(sent.shape, BF16),
            dma((chips,)),
            dma((chips,)),
            dma((chips,)),
            dma((chips,)),
            dma((count,)),
            dma((count,)),
            dma((count,)),
            dma((count,)),
        ],
        compiler_params=pltpu.CompilerParams(
            collective_id=2 * layer + 1, has_side_effects=True, vmem_limit_bytes=VMEM_LIMIT
        ),
        cost_estimate=SMALL,
    )(gated, gain, weight, hidden, sent)


def rotate(array, offset, count):
    return lax.ppermute(array, "col", [(c, (c + offset) % count) for c in range(count)])


def local(
    hidden_states,
    input_gain,
    inner_weight,
    proj_weight,
    step_weight,
    inner_kernel,
    proj_kernel,
    step_bias,
    decay_log,
    skip_gain,
    norm_gain,
    out_weight,
    inner_cache,
    proj_cache,
    state_cache,
    accepted,
    owners,
    tenant_ranges,
):
    layers = inner_weight.shape[0]
    row_width = inner_weight.shape[1]
    inner = inner_weight.shape[3]
    heads = step_weight.shape[2]
    size = inner // heads
    state = proj_weight.shape[2] // 2
    requests = state_cache.shape[1]
    row_count = lax.axis_size("row")
    col_count = lax.axis_size("col")
    model_width = row_width * row_count
    inner_width = inner * col_count
    me = lax.axis_index("col")
    ids = jnp.arange(requests, dtype=jnp.int32)
    request_ids = lax.axis_index("row") * requests + ids
    live = jnp.any(
        (request_ids[:, None] >= tenant_ranges[None, :, 0])
        & (request_ids[:, None] < tenant_ranges[None, :, 1]),
        axis=1,
    ).astype(jnp.int32)
    earlier = (owners[:, None] == owners[None, :]) & (ids[None, :] < ids[:, None])
    ranks = jnp.sum(earlier.astype(jnp.int32), axis=1)
    slots = lax.rem(owners - me + col_count, col_count) * SEND_CAP + ranks
    grid = jnp.arange(col_count * SEND_CAP, dtype=jnp.int32)
    slot_requests = jnp.sum(
        jnp.where(slots[None, :] == grid[:, None], ids[None, :], 0), axis=1
    ).astype(jnp.int32)
    mine = slot_requests[:SEND_CAP]

    picked = pick_states(slot_requests, state_cache, col_count)
    hidden, picked = lax.optimization_barrier((hidden_states, picked))
    picked = list(picked)
    starts = [picked[0]] + [None] * (col_count - 1)

    def turn_of(offset):
        if offset % 8 in (1, 7):
            return 0
        return 1 if offset % 8 in (2, 4, 6) else 2

    def send_turn(turn, after):
        offsets = [offset for offset in range(1, col_count) if turn_of(offset) == turn]
        blocks = [picked[offset] for offset in offsets]
        if after is not None:
            after, blocks = lax.optimization_barrier((after, blocks))
        for offset, block in zip(offsets, blocks):
            starts[offset] = rotate(block, offset, col_count)
        return after

    send_turn(0, None)
    early = [offset for offset in range(1, col_count) if turn_of(offset) == 0]
    hidden, arrived = lax.optimization_barrier((hidden, [starts[offset] for offset in early]))
    for offset, block in zip(early, arrived):
        starts[offset] = block
    head_rows = jnp.pad(
        jnp.stack([step_bias, decay_log, skip_gain], axis=1), ((0, 0), (0, 5), (0, 0))
    )
    states = None
    weight_layers = []
    b_layers = []
    for layer in range(layers):
        weight = jnp.concatenate(
            [
                inner_weight[layer].reshape(row_width, 2 * inner),
                proj_weight[layer],
                step_weight[layer],
                jnp.zeros((row_width, LANES - heads), BF16),
            ],
            axis=1,
        )
        proj = project(
            layer, col_count, row_count, heads, hidden, input_gain[layer : layer + 1], weight
        )
        if layer == 0:
            proj = send_turn(1, proj)
        if layer == layers - 1:
            proj = send_turn(2, proj)
        states, gated, sent, b_half = scan_layer(
            layer, model_width, col_count, slots, accepted, live, proj, inner_cache, proj_cache,
            inner_kernel, proj_kernel, head_rows, state_cache, states,
        )
        b_layers.append(b_half)
        hidden, received = output(
            layer, col_count, row_count, inner_width, gated, norm_gain[layer : layer + 1],
            out_weight[layer], hidden,
            sent.reshape(col_count, SEND_CAP, S, inner + LANES),
        )
        weight_layers.append(received)
    owned = owned_states(
        mine, jnp.stack(weight_layers), jnp.stack(b_layers), starts, layers, heads, size, state
    )
    return (hidden, states, owned)


def solution(mesh):
    placed = (
        P("col", "row"),
        P(None, "row"),
        P(None, "row", None, "col"),
        P(None, "row", None),
        P(None, "row", "col"),
        P(None, None, "col"),
        P(),
        P(None, "col"),
        P(None, "col"),
        P(None, "col"),
        P(None, "col"),
        P(None, "col", "row"),
        P(None, "row", None, "col"),
        P(None, "row", None, None),
        P(None, "row", "col", None, None),
        P("row"),
        P("row"),
        P(),
    )
    return jax.shard_map(
        local,
        mesh=mesh,
        in_specs=placed,
        out_specs=(
            P("col", "row"),
            P(None, "row", None, "col", None, None),
            P("row", "col", None, None, None, None, None),
        ),
        check_vma=False,
    )
```
